32 devices in a mesh: seq: 2 (over x), fsdp: 16 (over z, y, core).
Axes of the slice: x: 2, y: 2, z: 4, core: 2. Of those that a mesh axis runs over, the one named last changes fastest.
Arguments:
- hidden: bfloat16 [512, 8192], P('seq', 'fsdp'), may hold values from -28 to 28
- q_weight: bfloat16 [2048, 8192], P('fsdp'), may hold values from -0.0625 to 0.0625
- kv_weight: bfloat16 [512, 8192], P(None, 'fsdp'), may hold values from -0.0625 to 0.0625
- d_attended: bfloat16 [512, 2048], P('seq', 'fsdp'), may hold values from -6 to 6
- doc_lengths: int32 [4], replicated, may hold values from 1 to 384, as said below
- prompt_pos: int32 [32], replicated, may hold values from 0 to 511, as said below
Outputs:
- attended: bfloat16 [512, 2048], P('seq', 'fsdp')
- prompt_grad: float32 [32, 8192], P('seq', 'fsdp')
The draws below stay inside these ranges and needn't reach their ends.
Inputs may be any that keep to these rules, and one draw needn't show every extreme that they name: `doc_lengths`: 4 document lengths in pack order that sum to 512; exactly one is 384, at a position that varies from draw to draw, and the others are at least 1. `prompt_pos`: for every block i of 256 rows, entries i * 16 to (i + 1) * 16 - 1 are distinct rows of that block in rising order; row 0 and row 511 are always among them.
All inputs are finite; a program needn't handle non-finite values.
Results may differ from the reference program's by a relative error of at most 0.017.
The reference program's roundings to bfloat16 on the way count: a program that leaves them out, or rounds other values in their place, can miss the bound.
Values may be sent and summed in bfloat16 or wider, within the bound.
No kernel may reach another device: no remote copies, remote signals or barrier semaphores. Data moves between devices by JAX's collectives and lax.ppermute only.
A program may use at most 64 MiB of HBM per device.

```python
import math
import jax
import jax.numpy as jnp
from jax import lax

D = 8192
HEAD_DIM = 128
GROUP = 8
T_DEV = 256
P_DEV = 16
NDOC = 4
HEADS = 16
KV_HEADS = 2
SEQ = 512
PROMPTS = 32
LONGEST = 384


def draw_hidden(key, part):
    normal_part = jnp.clip(jax.random.normal(jax.random.fold_in(key, 11), (SEQ, D), jnp.float32), -6.0, 6.0)
    return normal_part.astype(jnp.bfloat16)


def draw_doc_lengths(key, part):
    remainder = SEQ - LONGEST
    cut_points = jnp.sort(jax.random.permutation(jax.random.fold_in(key, 31), remainder - 1)[:2]).astype(jnp.int32) + 1
    others = jnp.stack([cut_points[0], cut_points[1] - cut_points[0], remainder - cut_points[1]]).astype(jnp.int32)
    longest_at = jax.random.randint(jax.random.fold_in(key, 32), (), 0, NDOC, dtype=jnp.int32)
    indices = jnp.arange(NDOC, dtype=jnp.int32)
    other_index = jnp.clip(indices - (indices > longest_at).astype(jnp.int32), 0, 2)
    picked = jnp.take(others, other_index)
    return jnp.where(indices == longest_at, LONGEST, picked).astype(jnp.int32)


def draw_prompt_pos(key, part):
    block_total = SEQ // T_DEV
    block_keys = jax.random.split(jax.random.fold_in(key, 21), block_total)

    def choose(block_key):
        return jnp.sort(jax.random.permutation(block_key, T_DEV)[:P_DEV])
    picked = jax.vmap(choose)(block_keys).astype(jnp.int32)
    picked = picked.at[0, 0].set(0)
    picked = picked.at[block_total - 1, P_DEV - 1].set(T_DEV - 1)
    offsets = (jnp.arange(block_total, dtype=jnp.int32) * T_DEV)[:, None]
    return (picked + offsets).reshape(-1)


def block_levels(own_key, dims, cuts, least, high):
    loudness = 1.0
    for axis_at, blocks in cuts:
        steps = jax.random.uniform(jax.random.fold_in(jax.random.fold_in(own_key, 6), axis_at), (blocks,), jnp.float32, least / len(cuts), high / len(cuts))
        loudness = loudness * jnp.repeat(jnp.exp(steps), dims[axis_at] // blocks).reshape((-1,) + (1,) * (len(dims) - 1 - axis_at))
    return loudness


def noise(key, shape, scale, reach, pieces=(), kind=jnp.bfloat16):
    level = block_levels(key, shape, pieces, -0.22, 0.18) if pieces else 1.0
    values = jax.random.normal(key, shape, jnp.float32) * scale * level
    return jnp.minimum(jnp.maximum(values, -reach), reach).astype(kind)


def setup_inputs(seed: int = 0) -> dict:
    streams_of = jax.random.split(jax.random.key(seed), 7)
    hidden = draw_hidden(jax.random.fold_in(streams_of[6], 71), 0)
    q_weight = noise(streams_of[1], (HEADS * HEAD_DIM, D), D ** -0.5, 0.0625, ((0, 16),))
    kv_weight = noise(streams_of[2], (2 * KV_HEADS * HEAD_DIM, D), D ** -0.5, 0.0625, ((1, 16),))
    d_attended = noise(streams_of[3], (SEQ, HEADS * HEAD_DIM), 1.0, 6.0, ((0, 2), (1, 16)))
    doc_lengths = draw_doc_lengths(jax.random.fold_in(streams_of[6], 71), 0)
    prompt_pos = draw_prompt_pos(jax.random.fold_in(streams_of[6], 71), 0)
    return {"hidden": hidden, "q_weight": q_weight, "kv_weight": kv_weight, "d_attended": d_attended, "doc_lengths": doc_lengths, "prompt_pos": prompt_pos}


rope_theta = 1000000.0

def locate(tokens, doc_lengths):
    doc_ends = jnp.cumsum(doc_lengths).astype(jnp.int32)
    segment = lax.optimization_barrier(jnp.sum((tokens[:, None] >= doc_ends[None, :]).astype(jnp.int32), axis=1)).astype(jnp.int32)
    doc_starts = doc_ends - doc_lengths
    picked = segment[:, None] == jnp.arange(doc_lengths.shape[0], dtype=jnp.int32)[None, :]
    opening = lax.optimization_barrier(jnp.sum(jnp.where(picked, doc_starts[None, :], 0), axis=1)).astype(jnp.int32)
    return (segment, tokens - opening)

def rotate(vectors, positions, factor):
    halfway = vectors.shape[-1] // 2
    steps_up = jnp.arange(halfway, dtype=jnp.float32)
    frequency = jnp.exp(steps_up * (-2.0 * math.log(rope_theta) / vectors.shape[-1]))
    angles = positions.astype(jnp.float32)[:, None] * frequency[None, :]
    cosine = jnp.cos(angles)
    sine_part = jnp.sin(angles)
    leading = vectors[..., :halfway]
    trailing = vectors[..., halfway:]
    return jnp.concatenate([leading * cosine - factor * trailing * sine_part, trailing * cosine + factor * leading * sine_part], axis=-1)

def reference(hidden, q_weight, kv_weight, d_attended, doc_lengths, prompt_pos):
    score_scale = 1.0 / math.sqrt(HEAD_DIM)
    all_tokens = jnp.arange(SEQ, dtype=jnp.int32)
    segment_all, place_all = locate(all_tokens, doc_lengths)
    q_pre = jnp.dot(hidden, q_weight.T, preferred_element_type=jnp.float32)
    query_all = rotate(q_pre.reshape(SEQ, HEADS, HEAD_DIM).transpose(1, 0, 2), place_all, 1.0).astype(jnp.bfloat16)
    kv_rounded = jnp.dot(hidden, kv_weight.T, preferred_element_type=jnp.float32).astype(jnp.bfloat16)
    kv_heads = kv_rounded.reshape(SEQ, KV_HEADS, 2, HEAD_DIM).transpose(2, 1, 0, 3)
    key_all = rotate(kv_heads[0].astype(jnp.float32), place_all, 1.0).astype(jnp.bfloat16)
    value_all = kv_heads[1]
    upstream_all = d_attended.reshape(SEQ, HEADS, HEAD_DIM).transpose(1, 0, 2)
    allowed = (segment_all[:, None] == segment_all[None, :]) & (all_tokens[None, :] <= all_tokens[:, None])
    prompt_place = jnp.take(place_all, prompt_pos)

    def one_head(inputs):
        head_query, upstream, head_index = inputs
        kv_index = head_index // GROUP
        head_keys = lax.dynamic_index_in_dim(key_all, kv_index, 0, keepdims=False)
        values = lax.dynamic_index_in_dim(value_all, kv_index, 0, keepdims=False)
        raw_scores = jnp.dot(head_query, head_keys.T, preferred_element_type=jnp.float32) * score_scale
        scores = jnp.where(allowed, raw_scores, -jnp.inf)
        exponent_terms = jnp.exp(scores - lax.optimization_barrier(jnp.max(scores, axis=1, keepdims=True)))
        attention_probs = (exponent_terms / lax.optimization_barrier(jnp.sum(exponent_terms, axis=1, keepdims=True))).astype(jnp.bfloat16)
        attended = jnp.dot(attention_probs, values, preferred_element_type=jnp.float32).astype(jnp.bfloat16)
        rowdot = lax.optimization_barrier(jnp.sum(upstream.astype(jnp.float32) * attended.astype(jnp.float32), axis=1))
        row_dprobs = jnp.dot(jnp.take(upstream, prompt_pos, axis=0), values.T, preferred_element_type=jnp.float32)
        row_probs = jnp.take(attention_probs, prompt_pos, axis=0).astype(jnp.float32)
        row_dscores = (row_probs * (row_dprobs - jnp.take(rowdot, prompt_pos)[:, None])).astype(jnp.bfloat16)
        col_probs = jnp.take(attention_probs, prompt_pos, axis=1)
        col_dprobs = jnp.dot(upstream, jnp.take(values, prompt_pos, axis=0).T, preferred_element_type=jnp.float32)
        col_dscores = (col_probs.astype(jnp.float32) * (col_dprobs - rowdot[:, None])).astype(jnp.bfloat16)
        query_grad = jnp.dot(row_dscores, head_keys, preferred_element_type=jnp.float32) * score_scale
        query_grad = rotate(query_grad, prompt_place, -1.0).astype(jnp.bfloat16)
        key_grad = jnp.dot(col_dscores.T, head_query, preferred_element_type=jnp.float32) * score_scale
        key_grad = rotate(key_grad, prompt_place, -1.0)
        value_grad = jnp.dot(col_probs.T, upstream, preferred_element_type=jnp.float32)
        return (attended, query_grad, key_grad, value_grad)
    head_ids = jnp.arange(HEADS, dtype=jnp.int32)
    attended, query_grad, key_grad, value_grad = lax.map(one_head, (query_all, upstream_all, head_ids))
    attended_out = attended.transpose(1, 0, 2).reshape(SEQ, HEADS * HEAD_DIM)
    dq_rows = query_grad.transpose(1, 0, 2).reshape(PROMPTS, HEADS * HEAD_DIM)
    key_total = lax.optimization_barrier(jnp.sum(key_grad.reshape(KV_HEADS, GROUP, PROMPTS, HEAD_DIM), axis=1))
    value_total = lax.optimization_barrier(jnp.sum(value_grad.reshape(KV_HEADS, GROUP, PROMPTS, HEAD_DIM), axis=1))
    dkv_rows = jnp.stack([key_total, value_total], axis=1).transpose(2, 0, 1, 3)
    dkv_rows = dkv_rows.reshape(PROMPTS, 2 * KV_HEADS * HEAD_DIM).astype(jnp.bfloat16)
    prompt_grad = jnp.dot(dq_rows, q_weight, preferred_element_type=jnp.float32) + jnp.dot(dkv_rows, kv_weight, preferred_element_type=jnp.float32)
    return (attended_out, prompt_grad)
```

```python
import functools
import math

import jax
import jax.numpy as jnp
from jax import lax
from jax.experimental import pallas as pl
from jax.experimental.pallas import tpu as pltpu
from jax.sharding import PartitionSpec as P

GROUP = 8
CORES = 2
CHUNKS = 2
rope_theta = 1000000.0
f32 = jnp.float32
bf16 = jnp.bfloat16
VMEM = pl.BlockSpec(memory_space=pltpu.VMEM)
SMEM = pl.BlockSpec(memory_space=pltpu.SMEM)


def ring_of(chips):
    ys = max(1, math.isqrt(chips // 2))
    while chips % ys:
        ys -= 1
    zs = chips // ys
    if ys == 1 or zs % 2:
        return list(range(chips))
    path = [z * ys for z in range(zs)]
    for at, z in enumerate(reversed(range(zs))):
        line = list(range(1, ys))
        path += [z * ys + y for y in (line if at % 2 == 0 else line[::-1])]
    return path


def openings(tokens, doc_lengths):
    ending = jnp.int32(0)
    opening = jnp.zeros_like(tokens)
    for at in range(doc_lengths.shape[0] - 1):
        ending = ending + doc_lengths[at]
        opening = jnp.where(tokens >= ending, ending, opening)
    return opening


def turn_tables(places, width):
    halfway = width // 2
    steps_up = jnp.arange(halfway, dtype=f32)
    frequency = jnp.exp(steps_up * (-2.0 * math.log(rope_theta) / width))
    frequency = jnp.concatenate([frequency, frequency])
    sign = jnp.where(jnp.arange(width) < halfway, -1.0, 1.0).astype(f32)
    angles = places.astype(f32)[:, None] * frequency[None, :]
    return jnp.cos(angles), sign[None, :] * jnp.sin(angles)


def nt(a, b):
    return lax.dot_general(a, b, (((1,), (1,)), ((), ())), preferred_element_type=f32)


def nn(a, b):
    return jnp.dot(a, b, preferred_element_type=f32)


def turned(u, cosine, sine):
    return u * cosine + pltpu.roll(u, u.shape[-1] // 2, 1) * sine


def attend_kernel(scale, seqs, qa, qb, row_c, row_s, row_lo, row_hi, col_token, key, value, upstream, own_prompt,
                  all_prompt, prompt_c, prompt_s, attended_ref, core_msg, *seq_msgs):
    width = key.shape[1]
    query = turned(qa[...] + qb[...], row_c[...], row_s[...]).astype(bf16)
    tokens = col_token[...]
    allowed = (tokens >= row_lo[...]) & (tokens <= row_hi[...])
    scores = jnp.where(allowed, nt(query, key[...]) * scale, -jnp.inf)
    terms = jnp.exp(scores - jnp.max(scores, axis=1, keepdims=True))
    probs = (terms / jnp.sum(terms, axis=1, keepdims=True)).astype(bf16)
    attended = nn(probs, value[...]).astype(bf16)
    attended_ref[...] = attended
    up = upstream[...]
    rowdot = jnp.sum(up.astype(f32) * attended.astype(f32), axis=1, keepdims=True)
    dscores = (probs.astype(f32) * (nt(up, value[...]) - rowdot)).astype(bf16)
    rows = up.shape[0]
    prompts = own_prompt.shape[0]
    row_pick = (own_prompt[...] == lax.broadcasted_iota(jnp.int32, (prompts, rows), 1)).astype(f32).astype(bf16)
    col_pick = (all_prompt[...] == tokens).astype(f32).astype(bf16)
    row_dscores = nn(row_pick, dscores).astype(bf16)
    dq = turned(nn(row_dscores, key[...]) * scale, prompt_c[0:prompts, :], -prompt_s[0:prompts, :])
    col_dscores = nt(col_pick, dscores).astype(bf16)
    col_probs = nt(col_pick, probs).astype(bf16)
    dk = turned(nn(col_dscores, query) * scale, prompt_c[...], -prompt_s[...])
    dv = nn(col_probs, up)
    core_msg[:, 0:width] = dq.astype(bf16).astype(f32)
    core_msg[:, width : 2 * width] = dk[0:prompts, :]
    core_msg[:, 2 * width : 3 * width] = dv[0:prompts, :]
    for at, ref in enumerate(seq_msgs):
        low = (at + 1) * prompts
        ref[:, 0:width] = dk[low : low + prompts, :]
        ref[:, width : 2 * width] = dv[low : low + prompts, :]


def project_kernel(blocks, first, *refs):
    refs = list(refs)
    mine_in, other_in = (None, None) if first else (refs.pop(0), refs.pop(0))
    mine_out, other_out = refs[-2:]
    for at in range(CHUNKS):
        total_m = total_o = None
        for block in range(blocks):
            chunk = refs[block * (CHUNKS + 2) + at][...]
            wm = refs[block * (CHUNKS + 2) + CHUNKS][...]
            wo = refs[block * (CHUNKS + 2) + CHUNKS + 1][...]
            pm, po = nt(chunk, wm), nt(chunk, wo)
            total_m = pm if total_m is None else total_m + pm
            total_o = po if total_o is None else total_o + po
        rows = total_m.shape[0]
        here = slice(at * rows, (at + 1) * rows)
        if not first:
            total_m = total_m + mine_in[here, :]
            total_o = total_o + other_in[here, :]
        mine_out[here, :] = total_m
        other_out[here, :] = total_o


def project(parts, sums):
    blocks = len(parts)
    operands = list(sums)
    for chunks, wm, wo in parts:
        operands += list(chunks) + [wm, wo]
    rows = sum(c.shape[0] for c in parts[0][0])
    heads = parts[0][1].shape[0]
    depth = parts[0][1].shape[1]
    return pl.pallas_call(
        functools.partial(project_kernel, blocks, not sums),
        out_shape=[jax.ShapeDtypeStruct((rows, heads), f32)] * 2,
        in_specs=[VMEM] * len(operands),
        out_specs=[VMEM] * 2,
        cost_estimate=pl.CostEstimate(
            flops=4 * rows * heads * depth * blocks, bytes_accessed=blocks * depth * (rows + 2 * heads) * 2, transcendentals=0
        ),
        name="project",
    )(*operands)


def cut_kernel(where, mine, theirs, *outs):
    for at, out in enumerate(outs):
        rows, cols = out.shape
        r = pl.ds(pl.multiple_of(where[2 * at] * rows, rows), rows)
        c = pl.ds(pl.multiple_of(where[2 * at + 1] * cols, cols), cols)
        out[...] = mine[r, c] + theirs[r, c]


def spread_kernel(chips, where, weight_mine, weight_other, core_msg, core_got, *refs):
    outs = refs[-chips:]
    got = refs[:-chips]
    width = weight_mine.shape[0]
    features = outs[0].shape[1] - 2 * width
    dq_mine = core_msg[:, 0:width].astype(bf16)
    dq_other = core_got[:, 0:width].astype(bf16)
    dkv = core_msg[:, width:] + core_got[:, width:]
    for ref in got:
        dkv = dkv + ref[...]
    for at, out in enumerate(outs):
        mine_at = pl.ds(pl.multiple_of(where[2 * at] * features, features), features)
        other_at = pl.ds(pl.multiple_of(where[2 * at + 1] * features, features), features)
        share = nn(dq_mine, weight_mine[:, mine_at]) + nn(dq_other, weight_other[:, other_at])
        out[:, 0:features] = share.astype(out.dtype)
        out[:, features:] = dkv.astype(out.dtype)


def close_kernel(per_group, where, kv_weight, mine, *refs):
    out = refs[-1]
    got = [mine[...]] + [ref[...].astype(f32) for ref in refs[:-1]]
    features = out.shape[1]
    span = mine.shape[1] - features
    total = functools.reduce(lambda a, b: a + b, [g[:, 0:features] for g in got])
    for at in range(len(got) // per_group):
        members = got[at * per_group : (at + 1) * per_group]
        dkv = functools.reduce(lambda a, b: a + b, [g[:, features:] for g in members]).astype(bf16)
        rows = pl.ds(pl.multiple_of(where[at] * span, span), span)
        total = total + nn(dkv, kv_weight[rows, :])
    out[...] = total


def per_device(hidden, q_weight, kv_weight, d_attended, doc_lengths, prompt_pos):
    seqs = lax.axis_size("seq")
    fsdp = lax.axis_size("fsdp")
    chips = fsdp // CORES
    rows, features = hidden.shape
    head_dim = q_weight.shape[0]
    span = 2 * head_dim
    groups = kv_weight.shape[0] // span
    per_group = GROUP // CORES
    prompts = prompt_pos.shape[0] // seqs
    seq_rank = lax.axis_index("seq")
    fsdp_rank = lax.axis_index("fsdp")
    chip = fsdp_rank // CORES
    core = fsdp_rank % CORES
    first_row = seq_rank * rows
    scale = 1.0 / math.sqrt(head_dim)

    def swap(x, ds, dp, dc):
        perm = []
        for s in range(seqs):
            for p in range(chips):
                for c in range(CORES):
                    perm.append(((s * chips + p) * CORES + c, ((s ^ ds) * chips + (p ^ dp)) * CORES + (c ^ dc)))
        return lax.ppermute(x, ("seq", "fsdp"), perm)

    path = ring_of(chips)

    def pass_on(x, step):
        perm = [(path[i] * CORES + c, path[(i + step) % chips] * CORES + c) for i in range(chips) for c in range(CORES)]
        return lax.ppermute(x, "fsdp", perm)

    height = rows // CHUNKS
    ring = {0: [hidden[h * height : (h + 1) * height] for h in range(CHUNKS)]}
    half = chips // 2
    for k in range(1, half):
        ring[k] = [pass_on(x, 1) for x in ring[k - 1]]
        ring[-k] = [pass_on(x, -1) for x in ring[-(k - 1)]]
    ring[half] = [pass_on(ring[half - 1][h], 1) if h < CHUNKS // 2 else pass_on(ring[-(half - 1)][h], -1) for h in range(CHUNKS)]

    cut = q_weight.reshape(head_dim, chips, CORES, features)
    give = lax.dynamic_index_in_dim(cut, 1 - core, 2, keepdims=False).reshape(head_dim, chips * features)
    weight_other = swap(give, 0, 0, 1)

    half_rows = rows // CORES
    part_rows = half_rows // per_group
    theirs = lax.dynamic_slice_in_dim(hidden, (1 - core) * half_rows, half_rows, 0)
    mine = lax.dynamic_slice_in_dim(hidden, core * half_rows, half_rows, 0)
    kv_theirs = swap(nt(theirs, kv_weight), 0, 0, 1)
    kv_mine = nt(mine, kv_weight)
    targets = chip ^ jnp.arange(chips, dtype=jnp.int32)
    where = jnp.stack([targets % per_group, targets // per_group], axis=1).reshape(-1)
    pieces = pl.pallas_call(
        cut_kernel,
        out_shape=[jax.ShapeDtypeStruct((part_rows, span), f32)] * chips,
        in_specs=[SMEM, VMEM, VMEM],
        out_specs=[VMEM] * chips,
        cost_estimate=pl.CostEstimate(flops=rows * span, bytes_accessed=rows * span * 8, transcendentals=0),
        name="cut",
    )(where, kv_mine, kv_theirs)
    kv_sum = pieces[0]
    for d in range(1, chips):
        kv_sum = kv_sum + swap(pieces[d], 0, d, 0)
    kv_part = kv_sum.astype(bf16)
    kv_half = jnp.concatenate([kv_part] + [swap(kv_part, 0, d, 0) for d in range(1, per_group)], axis=0)
    offsets = [(e, c) for e in range(seqs) for c in range(CORES)]
    kv_all = jnp.concatenate([kv_half] + [swap(kv_half, e, 0, c) for e, c in offsets[1:]], axis=0)
    place_in = jnp.arange(half_rows, dtype=jnp.int32)
    within = ((chip % per_group) ^ (place_in // part_rows)) * part_rows + place_in % part_rows
    col_token = jnp.concatenate([(seq_rank ^ e) * rows + (core ^ c) * half_rows + within for e, c in offsets])
    key_c, key_s = turn_tables(col_token - openings(col_token, doc_lengths), head_dim)
    key_in = kv_all[:, :head_dim].astype(f32)
    key_turn = jnp.concatenate([key_in[:, head_dim // 2 :], key_in[:, : head_dim // 2]], axis=1)
    key = (key_in * key_c + key_turn * key_s).astype(bf16)
    value = kv_all[:, head_dim:]

    position = jnp.zeros((chips,), jnp.int32).at[jnp.array(path)].set(jnp.arange(chips, dtype=jnp.int32))
    spot = lax.dynamic_index_in_dim(position, chip, 0, keepdims=False)
    path_table = jnp.array(path, jnp.int32)

    def part(k):
        source = lax.dynamic_index_in_dim(path_table, (spot - k + chips) % chips, 0, keepdims=False)
        wm = lax.dynamic_slice_in_dim(q_weight, (source * CORES + core) * features, features, 1)
        wo = lax.dynamic_slice_in_dim(weight_other, source * features, features, 1)
        return (ring[k], wm, wo)

    sums = project([part(0)], [])
    for k in range(1, half):
        sums = project([part(k), part(-k)], sums)
    q_mine, q_other = project([part(half)], sums)
    q_got = swap(q_other, 0, 0, 1)

    row_token = first_row + jnp.arange(rows, dtype=jnp.int32)
    row_lo = openings(row_token, doc_lengths)
    row_c, row_s = turn_tables(row_token - row_lo, head_dim)
    by_seq = prompt_pos.reshape(seqs, prompts)
    ordered = jnp.concatenate(
        [lax.dynamic_index_in_dim(by_seq, seq_rank ^ e, 0, keepdims=False) for e in range(seqs)]
    )
    prompt_c, prompt_s = turn_tables(ordered - openings(ordered, doc_lengths), head_dim)
    own_prompt = ordered[:prompts] - first_row
    total = rows * seqs
    results = pl.pallas_call(
        functools.partial(attend_kernel, scale, seqs),
        out_shape=[
            jax.ShapeDtypeStruct((rows, head_dim), bf16),
            jax.ShapeDtypeStruct((prompts, 3 * head_dim), f32),
        ]
        + [jax.ShapeDtypeStruct((prompts, span), f32)] * (seqs - 1),
        in_specs=[VMEM] * 14,
        out_specs=[VMEM] * (seqs + 1),
        compiler_params=pltpu.CompilerParams(vmem_limit_bytes=(8 << 20) + 48 * rows * total),
        cost_estimate=pl.CostEstimate(
            flops=8 * rows * total * head_dim, bytes_accessed=8 * rows * head_dim * 4, transcendentals=rows * total
        ),
        name="attend",
    )(
        q_mine, q_got, row_c, row_s, row_lo[:, None], row_token[:, None], col_token[None, :], key, value, d_attended,
        own_prompt[:, None], ordered[:, None], prompt_c, prompt_s,
    )
    attended, core_msg, seq_msgs = results[0], results[1], results[2:]

    core_got = swap(core_msg, 0, 0, 1)
    seq_got = [swap(seq_msgs[e - 1], e, 0, c) for e, c in offsets if e]
    where = jnp.stack([targets * CORES + core, targets], axis=1).reshape(-1)
    shape = (prompts, features + span)
    shares = pl.pallas_call(
        functools.partial(spread_kernel, chips),
        out_shape=[jax.ShapeDtypeStruct(shape, f32)] + [jax.ShapeDtypeStruct(shape, bf16)] * (chips - 1),
        in_specs=[SMEM] + [VMEM] * (4 + len(seq_got)),
        out_specs=[VMEM] * chips,
        cost_estimate=pl.CostEstimate(
            flops=4 * prompts * head_dim * features * chips, bytes_accessed=head_dim * features * chips * 6, transcendentals=0
        ),
        name="spread",
    )(where, q_weight, weight_other, core_msg, core_got, *seq_got)
    got = [swap(shares[d], 0, d, 0) for d in range(1, chips)]
    group_at = (chip // per_group) ^ jnp.arange(groups, dtype=jnp.int32)
    prompt_grad = pl.pallas_call(
        functools.partial(close_kernel, per_group),
        out_shape=jax.ShapeDtypeStruct((prompts, features), f32),
        in_specs=[SMEM] + [VMEM] * (2 + len(got)),
        out_specs=VMEM,
        cost_estimate=pl.CostEstimate(
            flops=2 * prompts * features * groups * span, bytes_accessed=features * groups * span * 2, transcendentals=0
        ),
        name="close",
    )(group_at, kv_weight, shares[0], *got)
    return (attended, prompt_grad)


def solution(mesh):
    placed = (P("seq", "fsdp"), P("fsdp", None), P(None, "fsdp"), P("seq", "fsdp"), P(), P())
    return jax.shard_map(
        per_device,
        mesh=mesh,
        in_specs=placed,
        out_specs=(P("seq", "fsdp"), P("seq", "fsdp")),
        check_vma=False,
    )
```
